32 devices in a mesh: parts: 2 (over y), wide: 4 (over x, core), narrow: 4 (over z).
Axes of the slice: x: 2, y: 2, z: 4, core: 2. Of those that a mesh axis runs over, the one named last changes fastest.
Arguments:
- hist_events: bfloat16 [8, 2048, 512], P(('parts', 'wide'), 'narrow'), parts along dimension 0, may hold values from -6 to 6
- query_events: bfloat16 [8, 1024, 512], P(('parts', 'wide'), 'narrow'), parts along dimension 0, may hold values from -6 to 6
- hist_lengths: int32 [8], P(('parts', 'wide')), parts along dimension 0, may hold values from 512 to 2048
- time_buckets: int32 [8, 2048], P(('parts', 'wide'), 'narrow'), parts along dimension 0, may hold values from 0 to 127
- w_key: bfloat16 [512, 1024], replicated, may hold values from -0.25 to 0.25
- w_query: bfloat16 [512, 1024], replicated, may hold values from -0.25 to 0.25
- bias_table: bfloat16 [128, 8], replicated, may hold values from -3 to 3
- out_gain: float32 [512], replicated, may hold values from 0.1 to 1.9
- w_out: bfloat16 [512, 512], replicated, may hold values from -0.25 to 0.25
Outputs:
- layer_out: bfloat16 [8, 1024, 512], P(('parts', 'wide'), 'narrow'), parts along dimension 0
The draws below stay inside these ranges and needn't reach their ends.
There are 2 independent parts, one for each index of `parts`. The reference program is written for one: setup_inputs(seed, part) draws one part's arguments, and reference() takes and returns one part's arrays. A program takes and returns all parts, laid end to end along the dimension named above; an argument that names none is the same for every part. Nothing has to cross between parts.
All inputs are finite; a program needn't handle non-finite values.
Results may differ from the reference program's by a relative error of at most 0.0048.
Values may be sent and summed in bfloat16 or wider, within the bound.
No kernel may reach another device: no remote copies, remote signals or barrier semaphores. Data moves between devices by JAX's collectives and lax.ppermute only.
A program may use at most 128 MiB of HBM per device.

```python
import math
import jax
import jax.numpy as jnp
from jax import lax

D = 512
HEADS = 8
BUCKETS = 128
USERS = 4
HIST = 2048
QUERIES = 1024


def place_ends(values, rng, low, largest):
    longest = values.shape.index(max(values.shape))
    spots = []
    for shift in (0, 1):
        where = [jax.random.randint(jax.random.fold_in(rng, axis), (), 0, length) for axis, length in enumerate(values.shape)]
        where[longest] = (where[longest] + shift) % values.shape[longest]
        spots.append(tuple(where))
    return values.at[spots[0]].set(low).at[spots[1]].set(largest)


def block_scale(own_key, extent, split, low, high):
    level, own = 1.0, jax.random.fold_in(own_key, 6)
    for axis_at, parts in split:
        steps = jnp.exp(jax.random.uniform(jax.random.fold_in(own, axis_at), (parts,), jnp.float32, low / len(split), high / len(split)))
        level = level * jnp.repeat(steps, extent[axis_at] // parts).reshape([-1 if axis == axis_at else 1 for axis in range(len(extent))])
    return level


def normal_values(own_key, shape, width, reach, shards=(), kind=jnp.bfloat16):
    gain = block_scale(own_key, shape, shards, -0.22, 0.18) if shards else 1.0
    drawn = jax.random.normal(own_key, shape, jnp.float32) * width * gain
    return jnp.minimum(jnp.maximum(drawn, -reach), reach).astype(kind)


def setup_inputs(seed: int = 0, part: int = 0) -> dict:
    key_list = jax.random.split(jax.random.key(seed), 10)
    part_keys = jax.random.split(jax.random.fold_in(key_list[9], part), 10)
    return {
        "hist_events": normal_values(part_keys[0], (USERS, HIST, D), 1.0, 6.0, ((0, 4), (1, 4))),
        "query_events": normal_values(part_keys[1], (USERS, QUERIES, D), 1.0, 6.0, ((0, 4), (1, 4))),
        "hist_lengths": place_ends(jax.random.randint(part_keys[2], (USERS,), HIST // 4, HIST + 1), jax.random.fold_in(part_keys[2], 1), HIST // 4, HIST).astype(jnp.int32),
        "time_buckets": place_ends(jax.random.randint(part_keys[3], (USERS, HIST), 0, BUCKETS), jax.random.fold_in(part_keys[3], 1), 0, BUCKETS - 1).astype(jnp.int32),
        "w_key": normal_values(key_list[4], (D, 2 * D), D ** -0.5, 0.25),
        "w_query": normal_values(key_list[5], (D, 2 * D), D ** -0.5, 0.25),
        "bias_table": normal_values(key_list[6], (BUCKETS, HEADS), 1.0, 3.0),
        "out_gain": jnp.clip(1.0 + 0.18 * jax.random.normal(key_list[7], (D,), jnp.float32), 0.1, 1.9),
        "w_out": normal_values(key_list[8], (D, D), D ** -0.5, 0.25),
    }


def user_output(history, queries_in, length, buckets, w_key, w_query, bias_table, out_gain, w_out):
    head_size = D // HEADS
    score_scale = 1.0 / math.sqrt(head_size)
    key_value = jnp.dot(history, w_key, preferred_element_type=jnp.float32)
    key_states = lax.optimization_barrier(jax.nn.silu(key_value[:, :D]).astype(jnp.bfloat16))
    value_states = lax.optimization_barrier(key_value[:, D:].astype(jnp.bfloat16))
    query_gate = jnp.dot(queries_in, w_query, preferred_element_type=jnp.float32)
    query_states = lax.optimization_barrier(jax.nn.silu(query_gate[:, :D]).astype(jnp.bfloat16))
    gate_states = jax.nn.silu(query_gate[:, D:])
    bias_keys = bias_table[buckets].astype(jnp.float32)
    block_rows = 128 if HIST % 128 == 0 else HIST
    blocks = HIST // block_rows
    query_heads = query_states.astype(jnp.float32).reshape(QUERIES, HEADS, head_size)
    key_blocks = key_states.astype(jnp.float32).reshape(blocks, block_rows, HEADS, head_size)
    value_blocks = value_states.astype(jnp.float32).reshape(blocks, block_rows, HEADS, head_size)
    bias_blocks = bias_keys.reshape(blocks, block_rows, HEADS)

    def absorb_block(running, item):
        key_block, value_block, bias_block, block_index = item
        scores = jnp.einsum('qhd,khd->hqk', query_heads, key_block, precision=lax.Precision.HIGHEST)
        scores = scores * score_scale + bias_block.T[:, None, :]
        position = block_index * block_rows + jnp.arange(block_rows, dtype=jnp.int32)
        live = (position < length).astype(jnp.float32)
        weights = lax.optimization_barrier((jax.nn.silu(scores) * live[None, None, :]).astype(jnp.bfloat16))
        contrib = jnp.einsum('hqk,khd->qhd', weights.astype(jnp.float32), value_block, precision=lax.Precision.HIGHEST)
        return (running + contrib, None)
    running, _ = lax.scan(absorb_block, jnp.zeros((QUERIES, HEADS, head_size), jnp.float32), (key_blocks, value_blocks, bias_blocks, jnp.arange(blocks, dtype=jnp.int32)))
    attended = running.reshape(QUERIES, D)
    center = lax.optimization_barrier(jnp.mean(attended, axis=-1, keepdims=True))
    spread = lax.optimization_barrier(jnp.mean(jnp.square(attended - center), axis=-1, keepdims=True))
    normed = (attended - center) * lax.rsqrt(spread + 1e-05)
    mixed = (normed * out_gain * gate_states).astype(jnp.bfloat16)
    return (queries_in.astype(jnp.float32) + jnp.dot(mixed, w_out, preferred_element_type=jnp.float32)).astype(jnp.bfloat16)

def reference(hist_events, query_events, hist_lengths, time_buckets, w_key, w_query, bias_table, out_gain, w_out):

    def one_user(item):
        history, queries_in, length, buckets = item
        return user_output(history, queries_in, length, buckets, w_key, w_query, bias_table, out_gain, w_out)
    return lax.map(one_user, (hist_events, query_events, hist_lengths, time_buckets))
```

```python
import functools
import math

import jax
import jax.numpy as jnp
from jax import lax
from jax.experimental import pallas as pl
from jax.experimental.pallas import tpu as pltpu
from jax.sharding import PartitionSpec as P

LANES = 128


def silu(x):
    half = 0.5 * x
    return half + half * jnp.tanh(half)


def pick(index, table):
    value = jnp.int32(table[0])
    for i, entry in enumerate(table[1:], 1):
        value = jnp.where(index == i, jnp.int32(entry), value)
    return value


def dot(a, b, dims=((1,), (0,))):
    return lax.dot_general(a, b, (dims, ((), ())), preferred_element_type=jnp.float32)


def project_queries(own_ref, other_ref, w_ref, states_ref, gates_ref, *, scale):
    rows, width = own_ref.shape
    both = dot(own_ref[...], w_ref[...])
    states_ref[:rows] = (silu(both[:, :width]).astype(jnp.bfloat16) * scale).astype(jnp.bfloat16)
    gates_ref[...] = silu(both[:, width:])
    other = dot(other_ref[...], w_ref[:, :width])
    states_ref[rows:] = (silu(other).astype(jnp.bfloat16) * scale).astype(jnp.bfloat16)


def attend(
    length_ref, *refs, heads, owners, offset, shard_rows, first, chosen
):
    refs = list(refs)
    hist = refs.pop(0)[...]
    buckets = refs.pop(0)[...]
    place = lax.axis_index("narrow")
    if chosen is not None:
        take_own = pick(place, chosen) == 1
        hist = jnp.where(take_own, refs.pop(0)[...], hist)
        buckets = jnp.where(take_own, refs.pop(0)[...], buckets)
    w_ref, table_ref, states_ref = refs[:3]
    out_ref = refs[-1]
    total_ref = None if first else refs[3]

    rows, width = hist.shape
    head_size = width // heads
    per_block = LANES // head_size
    q_rows = states_ref.shape[0]
    q_block = min(256, q_rows)

    start = pick(place, owners) * shard_rows + offset
    live = (start + lax.broadcasted_iota(jnp.int32, (rows, 1), 0) < length_ref[0]).astype(jnp.float32)
    key_value = dot(hist, w_ref[...])
    keys = silu(key_value[:, :width]).astype(jnp.bfloat16)
    values = (key_value[:, width:] * live).astype(jnp.bfloat16)

    size = table_ref.shape[0]
    hot = lax.broadcasted_iota(jnp.int32, (size, rows), 0) == buckets
    table = jnp.concatenate(
        [table_ref[...] * 0.5, jnp.zeros((size, LANES - heads), jnp.bfloat16)], axis=1
    ).astype(jnp.bfloat16)
    bias = dot(hot.astype(jnp.bfloat16), table, ((0,), (0,))).astype(jnp.bfloat16)

    lane = lax.broadcasted_iota(jnp.int32, (1, LANES), 1)
    for block in range(width // LANES):
        cols = slice(block * LANES, (block + 1) * LANES)
        keys_bias = jnp.concatenate([keys[:, cols], bias], axis=1)
        parts = []
        for j in range(per_block):
            mask = ((lane // head_size) == j).astype(jnp.bfloat16)
            pointer = jnp.broadcast_to(
                (lane == block * per_block + j).astype(jnp.bfloat16), (q_block, LANES)
            )
            parts.append((mask, pointer, values[:, cols] * mask))
        for at in range(0, q_rows, q_block):
            queries = states_ref[at : at + q_block, cols]
            total = None
            for mask, pointer, value in parts:
                scores = dot(
                    jnp.concatenate([queries * mask, pointer], axis=1), keys_bias, ((1,), (1,))
                )
                weights = (scores + scores * jnp.tanh(scores)).astype(jnp.bfloat16)
                term = dot(weights, value)
                total = term if total is None else total + term
            if not first:
                total = total + total_ref[at : at + q_block, cols]
            out_ref[at : at + q_block, cols] = total.astype(out_ref.dtype)


def finish(total_ref, other_ref, gates_ref, gain_ref, w_ref, events_ref, out_ref):
    attended = total_ref[...] + other_ref[...].astype(jnp.float32)
    center = jnp.mean(attended, axis=-1, keepdims=True)
    away = attended - center
    spread = jnp.mean(away * away, axis=-1, keepdims=True)
    normed = away * lax.rsqrt(spread + 1e-05)
    mixed = (normed * gain_ref[...] * gates_ref[...]).astype(jnp.bfloat16)
    out_ref[...] = (events_ref[...].astype(jnp.float32) + dot(mixed, w_ref[...])).astype(jnp.bfloat16)


VMEM = pl.BlockSpec(memory_space=pltpu.VMEM)
SMEM = pl.BlockSpec(memory_space=pltpu.SMEM)
PARAMS = pltpu.CompilerParams(vmem_limit_bytes=40 * 1024 * 1024)


def routes(n):
    half = n // 2
    rank = [z if z < half else n - 1 - z for z in range(n)]

    def shard(z, step):
        own_half = (z < half) == (rank[z] % 2 == 0)
        at = (rank[z] + step) % half
        return at if own_half else n - 1 - at

    sources = []
    for step in range(half):
        row = []
        for z in range(n):
            source = shard(z, step)
            row.append(source if z < half else n - 1 - shard(n - 1 - z, step))
        sources.append(row)
    return rank, sources


def on_device(
    hist_events, query_events, hist_lengths, time_buckets, w_key, w_query, bias_table, out_gain, w_out, *, n
):
    history, queries_in, buckets = hist_events[0], query_events[0], time_buckets
    shard_rows, width = history.shape
    q_rows = queries_in.shape[0]
    heads = bias_table.shape[1]
    scale = 0.5 / math.sqrt(width // heads)
    rank, sources = routes(n)
    swap = [(z, z ^ 1) for z in range(n)]

    def send(x, step):
        pairs = [(source, z) for z, source in enumerate(sources[step]) if source != z]
        return lax.ppermute(x, "narrow", pairs)

    pieces = []
    for step in range(n // 2):
        parts = 2 if step == n // 2 - 1 else 1
        size = shard_rows // parts
        for part in range(parts):
            at = part * size
            pieces.append((step, at, size))
    received = [
        (send(history[at : at + size], step), send(buckets[:, at : at + size], step))
        for step, at, size in pieces
    ]
    other_queries = lax.ppermute(queries_in, "narrow", swap)

    states, gates = pl.pallas_call(
        functools.partial(project_queries, scale=scale),
        out_shape=(
            jax.ShapeDtypeStruct((2 * q_rows, width), jnp.bfloat16),
            jax.ShapeDtypeStruct((q_rows, width), jnp.float32),
        ),
        in_specs=[VMEM] * 3,
        out_specs=[VMEM] * 2,
        compiler_params=PARAMS,
        name="project_queries",
    )(queries_in, other_queries, w_query)

    def absorb(index, states, total, dtype, name):
        step, at, size = pieces[index]
        operands = [hist_lengths, *received[index]]
        chosen = None
        if step == 0:
            chosen = [int(sources[0][z] == z) for z in range(n)]
            operands += [history, buckets]
        operands += [w_key, bias_table, states]
        if total is not None:
            operands.append(total)
        body = functools.partial(
            attend,
            heads=heads,
            owners=sources[step],
            offset=at,
            shard_rows=shard_rows,
            first=total is None,
            chosen=chosen,
        )
        return pl.pallas_call(
            body,
            out_shape=jax.ShapeDtypeStruct((states.shape[0], width), dtype),
            in_specs=[SMEM] + [VMEM] * (len(operands) - 1),
            out_specs=VMEM,
            compiler_params=PARAMS,
            name=name,
        )(*operands)

    total = None
    for index in range(len(pieces) - 1):
        total = absorb(index, states, total, jnp.float32, f"attend_piece{index}")
    last = len(pieces) - 1
    theirs = absorb(last, states[q_rows:], total[q_rows:], jnp.bfloat16, "attend_theirs")
    theirs = lax.ppermute(theirs, "narrow", swap)
    own = absorb(last, states[:q_rows], total[:q_rows], jnp.float32, "attend_own")
    result = pl.pallas_call(
        finish,
        out_shape=jax.ShapeDtypeStruct((q_rows, width), jnp.bfloat16),
        in_specs=[VMEM] * 6,
        out_specs=VMEM,
        compiler_params=PARAMS,
        name="finish",
    )(own, theirs, gates, out_gain[None], w_out, queries_in)
    return result[None]


def solution(mesh):
    in_specs = (
        P(("parts", "wide"), "narrow", None),
        P(("parts", "wide"), "narrow", None),
        P(("parts", "wide")),
        P(("parts", "wide"), "narrow"),
        P(),
        P(),
        P(),
        P(),
        P(),
    )
    out_specs = P(("parts", "wide"), "narrow", None)
    return jax.shard_map(
        functools.partial(on_device, n=mesh.shape["narrow"]),
        mesh=mesh,
        in_specs=in_specs,
        out_specs=out_specs,
        check_vma=False,
    )
```

```python
import functools
import math

import jax
import jax.numpy as jnp
from jax import lax
from jax.experimental import pallas as pl
from jax.experimental.pallas import tpu as pltpu
from jax.sharding import PartitionSpec as P

LANES = 128


def silu(x):
    half = 0.5 * x
    return half + half * jnp.tanh(half)


def pick(index, table):
    value = jnp.int32(table[0])
    for i, entry in enumerate(table[1:], 1):
        value = jnp.where(index == i, jnp.int32(entry), value)
    return value


def dot(a, b, dims=((1,), (0,))):
    return lax.dot_general(a, b, (dims, ((), ())), preferred_element_type=jnp.float32)


def project_queries(own_ref, other_ref, w_ref, states_ref, gates_ref, *, scale):
    rows, width = own_ref.shape
    both = dot(own_ref[...], w_ref[...])
    states_ref[:rows] = (silu(both[:, :width]).astype(jnp.bfloat16) * scale).astype(jnp.bfloat16)
    gates_ref[...] = silu(both[:, width:])
    other = dot(other_ref[...], w_ref[:, :width])
    states_ref[rows:] = (silu(other).astype(jnp.bfloat16) * scale).astype(jnp.bfloat16)


def attend(
    length_ref, *refs, heads, owners, at, rows, q_at, q_rows, shard_rows, first, chosen
):
    refs = list(refs)
    hist_ref = refs.pop(0)
    hist = hist_ref[:rows]
    width = hist.shape[1]
    place = lax.axis_index("narrow")
    if chosen is not None:
        labels_ref, own_ref, own_labels_ref = refs.pop(0), refs.pop(0), refs.pop(0)
        from_row, from_col = labels_ref.shape[0] - 16 + at // width, at % width
        labels = labels_ref[:, from_col : from_col + rows].astype(jnp.float32)
        labels = labels[from_row : from_row + 1].astype(jnp.int32)
        take_own = pick(place, chosen) == 1
        hist = jnp.where(take_own, own_ref[at : at + rows], hist)
        labels = jnp.where(take_own, own_labels_ref[:, at : at + rows], labels)
    else:
        labels = refs.pop(0)[...]
    w_ref, table_ref, states_ref = refs[:3]
    out_ref = refs[-1]
    total_ref = None if first else refs[3]

    head_size = width // heads
    per_block = LANES // head_size
    q_block = min(256, q_rows)

    start = pick(place, owners) * shard_rows + at
    live = (start + lax.broadcasted_iota(jnp.int32, (rows, 1), 0) < length_ref[0]).astype(jnp.float32)
    key_value = dot(hist, w_ref[...])
    keys = silu(key_value[:, :width]).astype(jnp.bfloat16)
    values = (key_value[:, width:] * live).astype(jnp.bfloat16)

    size = table_ref.shape[0]
    hot = lax.broadcasted_iota(jnp.int32, (size, rows), 0) == labels
    table = jnp.concatenate(
        [table_ref[...] * 0.5, jnp.zeros((size, LANES - heads), jnp.bfloat16)], axis=1
    ).astype(jnp.bfloat16)
    bias = dot(hot.astype(jnp.bfloat16), table, ((0,), (0,))).astype(jnp.bfloat16)

    lane = lax.broadcasted_iota(jnp.int32, (1, LANES), 1)
    for block in range(width // LANES):
        cols = slice(block * LANES, (block + 1) * LANES)
        keys_bias = jnp.concatenate([keys[:, cols], bias], axis=1)
        parts = []
        for j in range(per_block):
            mask = ((lane // head_size) == j).astype(jnp.bfloat16)
            pointer = jnp.broadcast_to(
                (lane == block * per_block + j).astype(jnp.bfloat16), (q_block, LANES)
            )
            parts.append((mask, pointer, values[:, cols] * mask))
        for q in range(0, q_rows, q_block):
            queries = states_ref[q_at + q : q_at + q + q_block, cols]
            total = None
            for mask, pointer, value in parts:
                scores = dot(
                    jnp.concatenate([queries * mask, pointer], axis=1), keys_bias, ((1,), (1,))
                )
                weights = (scores + scores * jnp.tanh(scores)).astype(jnp.bfloat16)
                term = dot(weights, value)
                total = term if total is None else total + term
            if not first:
                total = total + total_ref[q_at + q : q_at + q + q_block, cols]
            out_ref[q : q + q_block, cols] = total.astype(out_ref.dtype)


def finish(total_ref, other_ref, gates_ref, gain_ref, w_ref, events_ref, out_ref):
    attended = total_ref[...] + other_ref[...].astype(jnp.float32)
    center = jnp.mean(attended, axis=-1, keepdims=True)
    away = attended - center
    spread = jnp.mean(away * away, axis=-1, keepdims=True)
    normed = away * lax.rsqrt(spread + 1e-05)
    mixed = (normed * gain_ref[...] * gates_ref[...]).astype(jnp.bfloat16)
    out_ref[...] = (events_ref[...].astype(jnp.float32) + dot(mixed, w_ref[...])).astype(jnp.bfloat16)


VMEM = pl.BlockSpec(memory_space=pltpu.VMEM)
SMEM = pl.BlockSpec(memory_space=pltpu.SMEM)
PARAMS = pltpu.CompilerParams(vmem_limit_bytes=16 * 1024 * 1024)


def routes(n):
    half = n // 2
    rank = [z if z < half else n - 1 - z for z in range(n)]

    def shard(z, step):
        own_half = (z < half) == (rank[z] % 2 == 0)
        at = (rank[z] + step) % half
        return at if own_half else n - 1 - at

    sources = []
    for step in range(half):
        row = []
        for z in range(n):
            source = shard(z, step)
            row.append(source if z < half else n - 1 - shard(n - 1 - z, step))
        sources.append(row)
    return rank, sources


def cost(flops, *arrays):
    return pl.CostEstimate(
        flops=flops,
        bytes_accessed=sum(a.size * a.dtype.itemsize for a in arrays),
        transcendentals=0,
    )


def on_device(
    hist_events, query_events, hist_lengths, time_buckets, w_key, w_query, bias_table, out_gain, w_out, *, n
):
    history, queries_in, buckets = hist_events[0], query_events[0], time_buckets
    shard_rows, width = history.shape
    q_rows = queries_in.shape[0]
    heads = bias_table.shape[1]
    scale = 0.5 / math.sqrt(width // heads)
    rank, sources = routes(n)
    swap = [(z, z ^ 1) for z in range(n)]

    def send(x, step):
        pairs = [(source, z) for z, source in enumerate(sources[step]) if source != z]
        return lax.ppermute(x, "narrow", pairs)

    half = shard_rows // 2
    pieces = [(step, 0, shard_rows) for step in range(1, n // 2)] + [(0, 0, half), (0, half, half)]
    received = {step: [send(history, step)] for step in range(1, n // 2)}
    tail = 16 * width
    bucket_rows = jnp.pad(buckets[0].astype(jnp.bfloat16), (0, tail - shard_rows)).reshape(16, width)
    head = jnp.concatenate([history[:half], bucket_rows])
    rest = history[half:]
    queries_out, labels, head, rest = lax.optimization_barrier((queries_in, buckets, head, rest))
    other_queries = lax.ppermute(queries_out, "narrow", swap)
    for step in range(1, n // 2):
        received[step].append(send(labels, step))
    head = send(head, 0)
    rest, received[1][0] = lax.optimization_barrier((rest, received[1][0]))
    rest = send(rest, 0)

    states, gates = pl.pallas_call(
        functools.partial(project_queries, scale=scale),
        out_shape=(
            jax.ShapeDtypeStruct((2 * q_rows, width), jnp.bfloat16),
            jax.ShapeDtypeStruct((q_rows, width), jnp.float32),
        ),
        in_specs=[VMEM] * 3,
        out_specs=[VMEM] * 2,
        compiler_params=PARAMS,
        cost_estimate=cost(6 * q_rows * width * width, queries_in, w_query),
        name="project_queries",
    )(queries_in, other_queries, w_query)

    def absorb(index, total, dtype, q_at, q_count, name):
        step, at, size = pieces[index]
        operands = [hist_lengths]
        chosen = None
        if step == 0:
            chosen = [int(sources[0][z] == z) for z in range(n)]
            operands += [rest if at else head, head, history, buckets]
        else:
            operands += received[step]
        operands += [w_key, bias_table, states]
        if total is not None:
            operands.append(total)
        body = functools.partial(
            attend,
            heads=heads,
            owners=sources[step],
            at=at,
            rows=size,
            q_at=q_at,
            q_rows=q_count,
            shard_rows=shard_rows,
            first=total is None,
            chosen=chosen,
        )
        return pl.pallas_call(
            body,
            out_shape=jax.ShapeDtypeStruct((q_count, width), dtype),
            in_specs=[SMEM] + [VMEM] * (len(operands) - 1),
            out_specs=VMEM,
            compiler_params=PARAMS,
            cost_estimate=cost(64 * q_count * size * width, *operands),
            name=name,
        )(*operands)

    total = None
    for index in range(len(pieces) - 1):
        total = absorb(index, total, jnp.float32, 0, 2 * q_rows, f"attend_piece{index}")
    last = len(pieces) - 1
    theirs = absorb(last, total, jnp.bfloat16, q_rows, q_rows, "attend_theirs")
    theirs = lax.ppermute(theirs, "narrow", swap)
    own = absorb(last, total, jnp.float32, 0, q_rows, "attend_own")
    result = pl.pallas_call(
        finish,
        out_shape=jax.ShapeDtypeStruct((q_rows, width), jnp.bfloat16),
        in_specs=[VMEM] * 6,
        out_specs=VMEM,
        compiler_params=PARAMS,
        cost_estimate=cost(2 * q_rows * width * width, own, w_out),
        name="finish",
    )(own, theirs, gates, out_gain[None], w_out, queries_in)
    return result[None]


def solution(mesh):
    in_specs = (
        P(("parts", "wide"), "narrow", None),
        P(("parts", "wide"), "narrow", None),
        P(("parts", "wide")),
        P(("parts", "wide"), "narrow"),
        P(),
        P(),
        P(),
        P(),
        P(),
    )
    out_specs = P(("parts", "wide"), "narrow", None)
    return jax.shard_map(
        functools.partial(on_device, n=mesh.shape["narrow"]),
        mesh=mesh,
        in_specs=in_specs,
        out_specs=out_specs,
        check_vma=False,
    )
```

```python
import functools
import math

import jax
import jax.numpy as jnp
from jax import lax
from jax.experimental import pallas as pl
from jax.experimental.pallas import tpu as pltpu
from jax.sharding import PartitionSpec as P

SPAN = 256


def silu(x):
    half = 0.5 * x
    return half + half * jnp.tanh(half)


def pick(index, table):
    value = jnp.int32(table[0])
    for i, entry in enumerate(table[1:], 1):
        value = jnp.where(index == i, jnp.int32(entry), value)
    return value


def dot(a, b, dims=((1,), (0,))):
    return lax.dot_general(a, b, (dims, ((), ())), preferred_element_type=jnp.float32)


def project_gates(events_ref, w_ref, w_key_ref, gates_ref):
    del w_key_ref
    width = events_ref.shape[1]
    gates_ref[...] = silu(dot(events_ref[...], w_ref[:, width:]))


def pack(history_ref, labels_ref, head_ref, rest_ref, sems):
    half, width = rest_ref.shape
    copies = [
        pltpu.make_async_copy(history_ref.at[:half], head_ref.at[:half], sems.at[0]),
        pltpu.make_async_copy(history_ref.at[half:], rest_ref, sems.at[1]),
    ]
    for copy in copies:
        copy.start()
    labels = labels_ref[...].astype(jnp.float32)
    for i, at in enumerate(range(0, labels.shape[1], width)):
        part = labels[:, at : at + width]
        row = half + 16 * i
        head_ref[row : row + 16, : part.shape[1]] = jnp.broadcast_to(
            part, (16, part.shape[1])
        ).astype(jnp.bfloat16)
    for copy in copies:
        copy.wait()


def attend(length_ref, *refs, heads, parts, owners, chosen, shard_rows, first, raw, keep, scale):
    refs = list(refs)
    kept_ref = refs.pop() if keep else None
    out_ref = refs.pop()
    total_ref = None if first else refs.pop()
    w_query_ref = refs.pop() if raw else None
    w_ref, table_ref, states_ref = refs[-3:]
    states = states_ref[...]
    if raw:
        states = silu(dot(states, w_query_ref[:, : states.shape[1]])).astype(jnp.bfloat16)
        states = (states * scale).astype(jnp.bfloat16)
    if keep:
        kept_ref[...] = states
    place = lax.axis_index("narrow")
    owner = pick(place, owners)
    total = total_ref
    for at, rows in parts:
        if chosen is None:
            hist_ref, labels_ref = refs[:2]
            hist, labels = hist_ref[at : at + rows], labels_ref[:, at : at + rows]
            width = hist.shape[1]
        else:
            take_own = pick(place, chosen) == 1
            hist_ref, own_ref = refs.pop(0), refs.pop(0)
            hist = jnp.where(take_own, own_ref[:rows], hist_ref[:rows])
            width = hist.shape[1]
            labels_ref, own_labels_ref = refs.pop(0), refs.pop(0)
            where = (
                slice(shard_rows // 2 + 16 * (at // width), shard_rows // 2 + 16 * (at // width) + 16),
                slice(at % width, at % width + rows),
            )
            labels = jnp.where(take_own, own_labels_ref[where], labels_ref[where])
            labels = labels.astype(jnp.float32)[:1].astype(jnp.int32)
        head_size = width // heads
        per_span = SPAN // head_size
        q_rows = states.shape[0]
        start = owner * shard_rows + at
        row = start + lax.broadcasted_iota(jnp.int32, (rows, 1), 0)
        live = (row < length_ref[0]).astype(jnp.float32)
        key_value = dot(hist, w_ref[...])
        keys = silu(key_value[:, :width]).astype(jnp.bfloat16)
        values = (key_value[:, width:] * live).astype(jnp.bfloat16)

        hot = lax.broadcasted_iota(jnp.int32, (table_ref.shape[1], rows), 0) == labels
        bias = dot(table_ref[...], hot.astype(jnp.bfloat16)) * 0.5

        lane = lax.broadcasted_iota(jnp.int32, (1, SPAN), 1) // head_size
        for block in range(width // SPAN):
            cols = slice(block * SPAN, (block + 1) * SPAN)
            queries = states[:, cols]
            stack = [queries * (lane == j).astype(jnp.bfloat16) for j in range(per_span)]
            scores = dot(jnp.concatenate(stack, axis=0), keys[:, cols], ((1,), (1,)))
            weights = []
            for j in range(per_span):
                h = block * per_span + j
                s = scores[j * q_rows : (j + 1) * q_rows] + bias[h : h + 1]
                weights.append((s + s * jnp.tanh(s)).astype(jnp.bfloat16))
            mixed = dot(jnp.concatenate(weights, axis=0), values[:, cols])
            term = mixed[:q_rows]
            for j in range(1, per_span):
                term = jnp.where(lane == j, mixed[j * q_rows : (j + 1) * q_rows], term)
            if total is not None:
                term = term + total[:, cols]
            out_ref[:, cols] = term.astype(out_ref.dtype)
        total = out_ref


def finish(total_ref, other_ref, gates_ref, gain_ref, w_ref, events_ref, out_ref):
    attended = total_ref[...] + other_ref[...].astype(jnp.float32)
    center = jnp.mean(attended, axis=-1, keepdims=True)
    away = attended - center
    spread = jnp.mean(away * away, axis=-1, keepdims=True)
    normed = away * lax.rsqrt(spread + 1e-05)
    mixed = (normed * gain_ref[...] * gates_ref[...]).astype(jnp.bfloat16)
    out_ref[...] = (events_ref[...].astype(jnp.float32) + dot(mixed, w_ref[...])).astype(jnp.bfloat16)


VMEM = pl.BlockSpec(memory_space=pltpu.VMEM)
SMEM = pl.BlockSpec(memory_space=pltpu.SMEM)
PARAMS = pltpu.CompilerParams(vmem_limit_bytes=12 * 1024 * 1024)


def routes(n):
    half = n // 2
    rank = [z if z < half else n - 1 - z for z in range(n)]

    def shard(z, step):
        own_half = (z < half) == (rank[z] % 2 == 0)
        at = (rank[z] + step) % half
        return at if own_half else n - 1 - at

    sources = []
    for step in range(half):
        row = []
        for z in range(n):
            source = shard(z, step)
            row.append(source if z < half else n - 1 - shard(n - 1 - z, step))
        sources.append(row)
    return rank, sources


def cost(flops, *arrays):
    return pl.CostEstimate(
        flops=flops,
        bytes_accessed=sum(a.size * a.dtype.itemsize for a in arrays),
        transcendentals=0,
    )


def on_device(
    hist_events, query_events, hist_lengths, time_buckets, w_key, w_query, bias_table, out_gain, w_out, *, n
):
    history, queries_in, buckets = hist_events[0], query_events[0], time_buckets
    shard_rows, width = history.shape
    q_rows = queries_in.shape[0]
    heads = bias_table.shape[1]
    scale = 0.5 / math.sqrt(width // heads)
    rank, sources = routes(n)
    swap = [(z, z ^ 1) for z in range(n)]

    def send(x, step):
        pairs = [(source, z) for z, source in enumerate(sources[step]) if source != z]
        return lax.ppermute(x, "narrow", pairs)

    half = shard_rows // 2
    pieces = [(step, at, half) for step in range(n // 2) for at in (0, half)]
    received = {step: [send(history, step)] for step in range(1, n // 2)}
    label_rows = 16 * (-(-shard_rows // width))
    head, rest = pl.pallas_call(
        pack,
        out_shape=(
            jax.ShapeDtypeStruct((half + label_rows, width), jnp.bfloat16),
            jax.ShapeDtypeStruct((half, width), jnp.bfloat16),
        ),
        in_specs=[pl.BlockSpec(memory_space=pl.ANY), VMEM],
        out_specs=[VMEM] * 2,
        scratch_shapes=[pltpu.SemaphoreType.DMA((2,))],
        compiler_params=PARAMS,
        name="pack",
    )(history, buckets)
    queries_out, labels, head_own, rest_own = lax.optimization_barrier(
        (queries_in, buckets, head, rest)
    )
    other_queries = lax.ppermute(queries_out, "narrow", swap)
    for step in range(1, n // 2):
        received[step].append(send(labels, step))
    head = send(head_own, 0)

    gates = pl.pallas_call(
        project_gates,
        out_shape=jax.ShapeDtypeStruct((q_rows, width), jnp.float32),
        in_specs=[VMEM] * 3,
        out_specs=VMEM,
        compiler_params=PARAMS,
        cost_estimate=cost(2 * q_rows * width * width, queries_in, w_query),
        name="project_gates",
    )(queries_in, w_query, w_key)
    rest_own, gates = lax.optimization_barrier((rest_own, gates))
    rest = send(rest_own, 0)

    def absorb(states, indices, total, dtype, name, raw=False, keep=False):
        step = pieces[indices[0]][0]
        parts = [pieces[index][1:] for index in indices]
        operands = [hist_lengths]
        chosen = None
        for at, _ in parts:
            if step == 0:
                chosen = [int(sources[0][z] == z) for z in range(n)]
                operands += [rest if at else head, rest_own if at else head_own, head, head_own]
        if step:
            operands += received[step]
        operands += [w_key, bias_table.T, states]
        if raw:
            operands.append(w_query)
        if total is not None:
            operands.append(total)
        body = functools.partial(
            attend,
            heads=heads,
            parts=parts,
            owners=sources[step],
            chosen=chosen,
            shard_rows=shard_rows,
            first=total is None,
            raw=raw,
            keep=keep,
            scale=scale,
        )
        rows = sum(size for _, size in parts)
        shape = jax.ShapeDtypeStruct((q_rows, width), dtype)
        kept = jax.ShapeDtypeStruct((q_rows, width), jnp.bfloat16)
        return pl.pallas_call(
            body,
            out_shape=(shape, kept) if keep else shape,
            in_specs=[SMEM] + [VMEM] * (len(operands) - 1),
            out_specs=[VMEM] * 2 if keep else VMEM,
            compiler_params=PARAMS,
            cost_estimate=cost(64 * q_rows * rows * width, *operands),
            name=name,
        )(*operands)

    own = None
    for step in range(1, n // 2):
        own = absorb(
            queries_in, [2 * step, 2 * step + 1], own, jnp.float32, f"own_far{step}", raw=True
        )
    other_queries, own = lax.optimization_barrier((other_queries, own))
    theirs, other_states = absorb(
        other_queries, [2, 3], None, jnp.float32, "theirs_far1", raw=True, keep=True
    )
    for step in range(2, n // 2):
        theirs = absorb(other_states, [2 * step, 2 * step + 1], theirs, jnp.float32, f"theirs_far{step}")
    theirs = absorb(other_states, [0], theirs, jnp.float32, "theirs_near0")
    theirs = absorb(other_states, [1], theirs, jnp.bfloat16, "theirs_near1")
    theirs_sent, own, rest = lax.optimization_barrier((theirs, own, rest))
    theirs = lax.ppermute(theirs_sent, "narrow", swap)
    own = absorb(queries_in, [0, 1], own, jnp.float32, "own_near", raw=True)
    result = pl.pallas_call(
        finish,
        out_shape=jax.ShapeDtypeStruct((q_rows, width), jnp.bfloat16),
        in_specs=[VMEM] * 6,
        out_specs=VMEM,
        compiler_params=PARAMS,
        cost_estimate=cost(2 * q_rows * width * width, own, w_out),
        name="finish",
    )(own, theirs, gates, out_gain[None], w_out, queries_in)
    return result[None]


def solution(mesh):
    in_specs = (
        P(("parts", "wide"), "narrow", None),
        P(("parts", "wide"), "narrow", None),
        P(("parts", "wide")),
        P(("parts", "wide"), "narrow"),
        P(),
        P(),
        P(),
        P(),
        P(),
    )
    out_specs = P(("parts", "wide"), "narrow", None)
    return jax.shard_map(
        functools.partial(on_device, n=mesh.shape["narrow"]),
        mesh=mesh,
        in_specs=in_specs,
        out_specs=out_specs,
        check_vma=False,
    )
```

```python
import functools
import math

import jax
import jax.numpy as jnp
from jax import lax
from jax.experimental import pallas as pl
from jax.experimental.pallas import tpu as pltpu
from jax.sharding import PartitionSpec as P

SPAN = 256


def silu(x):
    half = 0.5 * x
    return half + half * jnp.tanh(half)


def pick(index, table):
    value = jnp.int32(table[0])
    for i, entry in enumerate(table[1:], 1):
        value = jnp.where(index == i, jnp.int32(entry), value)
    return value


def dot(a, b, dims=((1,), (0,))):
    return lax.dot_general(a, b, (dims, ((), ())), preferred_element_type=jnp.float32)


def project_gates(events_ref, w_ref, w_key_ref, gates_ref):
    del w_key_ref
    width = events_ref.shape[1]
    gates_ref[...] = silu(dot(events_ref[...], w_ref[:, width:]))


def pack(history_ref, labels_ref, head_ref, rest_ref, sems):
    half, width = rest_ref.shape
    copies = [
        pltpu.make_async_copy(history_ref.at[:half], head_ref.at[:half], sems.at[0]),
        pltpu.make_async_copy(history_ref.at[half:], rest_ref, sems.at[1]),
    ]
    for copy in copies:
        copy.start()
    labels = labels_ref[...].astype(jnp.float32)
    for i, at in enumerate(range(0, labels.shape[1], width)):
        part = labels[:, at : at + width]
        row = half + 16 * i
        head_ref[row : row + 16, : part.shape[1]] = jnp.broadcast_to(
            part, (16, part.shape[1])
        ).astype(jnp.bfloat16)
    for copy in copies:
        copy.wait()


def attend(length_ref, *refs, heads, parts, owners, chosen, shard_rows, first, raw, keep, save, given, scale):
    refs = list(refs)
    saved = [refs.pop() for _ in range(3)] if save else None
    kept_ref = refs.pop() if keep else None
    out_ref = refs.pop()
    total_ref = None if first else refs.pop()
    w_query_ref = refs.pop() if raw else None
    states = refs.pop()[...]
    if not given:
        table_ref, w_ref = refs.pop(), refs.pop()
    if raw:
        states = silu(dot(states, w_query_ref[:, : states.shape[1]])).astype(jnp.bfloat16)
        states = (states * scale).astype(jnp.bfloat16)
    if keep:
        kept_ref[...] = states
    place = lax.axis_index("narrow")
    owner = pick(place, owners)
    total = total_ref
    for at, rows in parts:
        if given:
            keys_ref, values_ref, bias_ref = refs
            keys, values = keys_ref[at : at + rows], values_ref[at : at + rows]
            bias = bias_ref[:, at : at + rows]
            width = keys.shape[1]
        elif chosen is None:
            hist_ref, labels_ref = refs
            hist, labels = hist_ref[at : at + rows], labels_ref[:, at : at + rows]
            width = hist.shape[1]
        else:
            take_own = pick(place, chosen) == 1
            hist = refs.pop(0)[:rows]
            if at:
                hist = jnp.where(lax.axis_index("wide") % 2 == 0, hist, refs.pop(0)[:rows])
            hist = jnp.where(take_own, refs.pop(0)[:rows], hist)
            width = hist.shape[1]
            labels_ref, own_labels_ref = refs.pop(0), refs.pop(0)
            where = (
                slice(shard_rows // 2 + 16 * (at // width), shard_rows // 2 + 16 * (at // width) + 16),
                slice(at % width, at % width + rows),
            )
            labels = jnp.where(take_own, own_labels_ref[where], labels_ref[where])
            labels = labels.astype(jnp.float32)[:1].astype(jnp.int32)
        head_size = width // heads
        per_span = SPAN // head_size
        q_rows = states.shape[0]
        if not given:
            start = owner * shard_rows + at
            row = start + lax.broadcasted_iota(jnp.int32, (rows, 1), 0)
            live = (row < length_ref[0]).astype(jnp.float32)
            key_value = dot(hist, w_ref[...])
            keys = silu(key_value[:, :width]).astype(jnp.bfloat16)
            values = (key_value[:, width:] * live).astype(jnp.bfloat16)
            hot = lax.broadcasted_iota(jnp.int32, (table_ref.shape[1], rows), 0) == labels
            bias = dot(table_ref[...], hot.astype(jnp.bfloat16)) * 0.5
        if save:
            saved[2][at : at + rows] = keys
            saved[1][at : at + rows] = values
            saved[0][:, at : at + rows] = bias

        lane = lax.broadcasted_iota(jnp.int32, (1, SPAN), 1) // head_size
        for block in range(width // SPAN):
            cols = slice(block * SPAN, (block + 1) * SPAN)
            queries = states[:, cols]
            stack = [queries * (lane == j).astype(jnp.bfloat16) for j in range(per_span)]
            scores = dot(jnp.concatenate(stack, axis=0), keys[:, cols], ((1,), (1,)))
            weights = []
            for j in range(per_span):
                h = block * per_span + j
                s = scores[j * q_rows : (j + 1) * q_rows] + bias[h : h + 1]
                weights.append((s + s * jnp.tanh(s)).astype(jnp.bfloat16))
            mixed = dot(jnp.concatenate(weights, axis=0), values[:, cols])
            term = mixed[:q_rows]
            for j in range(1, per_span):
                term = jnp.where(lane == j, mixed[j * q_rows : (j + 1) * q_rows], term)
            if total is not None:
                term = term + total[:, cols]
            out_ref[:, cols] = term.astype(out_ref.dtype)
        total = out_ref


def finish(total_ref, other_ref, gates_ref, gain_ref, w_ref, events_ref, out_ref):
    attended = total_ref[...] + other_ref[...].astype(jnp.float32)
    center = jnp.mean(attended, axis=-1, keepdims=True)
    away = attended - center
    spread = jnp.mean(away * away, axis=-1, keepdims=True)
    normed = away * lax.rsqrt(spread + 1e-05)
    mixed = (normed * gain_ref[...] * gates_ref[...]).astype(jnp.bfloat16)
    out_ref[...] = (events_ref[...].astype(jnp.float32) + dot(mixed, w_ref[...])).astype(jnp.bfloat16)


VMEM = pl.BlockSpec(memory_space=pltpu.VMEM)
SMEM = pl.BlockSpec(memory_space=pltpu.SMEM)
PARAMS = pltpu.CompilerParams(vmem_limit_bytes=12 * 1024 * 1024)


def routes(n):
    half = n // 2
    rank = [z if z < half else n - 1 - z for z in range(n)]

    def shard(z, step):
        own_half = (z < half) == (rank[z] % 2 == 0)
        at = (rank[z] + step) % half
        return at if own_half else n - 1 - at

    sources = []
    for step in range(half):
        row = []
        for z in range(n):
            source = shard(z, step)
            row.append(source if z < half else n - 1 - shard(n - 1 - z, step))
        sources.append(row)
    return rank, sources


def cost(flops, *arrays):
    return pl.CostEstimate(
        flops=flops,
        bytes_accessed=sum(a.size * a.dtype.itemsize for a in arrays),
        transcendentals=0,
    )


def on_device(
    hist_events, query_events, hist_lengths, time_buckets, w_key, w_query, bias_table, out_gain, w_out, *, n, wide
):
    history, queries_in, buckets = hist_events[0], query_events[0], time_buckets
    shard_rows, width = history.shape
    q_rows = queries_in.shape[0]
    heads = bias_table.shape[1]
    scale = 0.5 / math.sqrt(width // heads)
    rank, sources = routes(n)
    swap = [(z, z ^ 1) for z in range(n)]

    def send(x, step, turn=None):
        pairs = [(source, z) for z, source in enumerate(sources[step]) if source != z]
        if turn is None:
            return lax.ppermute(x, "narrow", pairs)
        lines = [i * n for i in range(wide) if i % 2 == turn]
        pairs = [(line + a, line + b) for line in lines for a, b in pairs]
        return lax.ppermute(x, ("wide", "narrow"), pairs)

    half = shard_rows // 2
    pieces = [(step, at, half) for step in range(n // 2) for at in (0, half)]
    received = {step: [send(history, step)] for step in range(1, n // 2)}
    label_rows = 16 * (-(-shard_rows // width))
    head, rest = pl.pallas_call(
        pack,
        out_shape=(
            jax.ShapeDtypeStruct((half + label_rows, width), jnp.bfloat16),
            jax.ShapeDtypeStruct((half, width), jnp.bfloat16),
        ),
        in_specs=[pl.BlockSpec(memory_space=pl.ANY), VMEM],
        out_specs=[VMEM] * 2,
        scratch_shapes=[pltpu.SemaphoreType.DMA((2,))],
        compiler_params=PARAMS,
        name="pack",
    )(history, buckets)
    queries_out, labels, head_own, rest_own = lax.optimization_barrier(
        (queries_in, buckets, head, rest)
    )
    other_queries = lax.ppermute(queries_out, "narrow", swap)
    for step in range(1, n // 2):
        received[step].append(send(labels, step))
    head = send(head_own, 0)

    gates = pl.pallas_call(
        project_gates,
        out_shape=jax.ShapeDtypeStruct((q_rows, width), jnp.float32),
        in_specs=[VMEM] * 3,
        out_specs=VMEM,
        compiler_params=PARAMS,
        cost_estimate=cost(2 * q_rows * width * width, queries_in, w_query),
        name="project_gates",
    )(queries_in, w_query, w_key)
    rest_own, gates = lax.optimization_barrier((rest_own, gates))
    rests = [send(rest_own, 0, 0)]

    def absorb(states, indices, total, dtype, name, raw=False, keep=False, save=False, given=None):
        step = pieces[indices[0]][0]
        parts = [pieces[index][1:] for index in indices]
        operands = [hist_lengths]
        chosen = None
        for at, _ in parts:
            if step == 0:
                chosen = [int(sources[0][z] == z) for z in range(n)]
                operands += [*rests, rest_own] if at else [head, head_own]
                operands += [head, head_own]
        if given is not None:
            operands += given
        elif step:
            operands += received[step]
        if given is None:
            operands += [w_key, bias_table.T]
        operands.append(states)
        if raw:
            operands.append(w_query)
        if total is not None:
            operands.append(total)
        body = functools.partial(
            attend,
            heads=heads,
            parts=parts,
            owners=sources[step],
            chosen=chosen,
            shard_rows=shard_rows,
            first=total is None,
            raw=raw,
            keep=keep,
            save=save,
            given=given is not None,
            scale=scale,
        )
        rows = sum(size for _, size in parts)
        shapes = [jax.ShapeDtypeStruct((q_rows, width), dtype)]
        if keep:
            shapes.append(jax.ShapeDtypeStruct((q_rows, width), jnp.bfloat16))
        if save:
            shapes += [jax.ShapeDtypeStruct((rows, width), jnp.bfloat16)] * 2
            shapes.append(jax.ShapeDtypeStruct((heads, rows), jnp.float32))
        return pl.pallas_call(
            body,
            out_shape=shapes,
            in_specs=[SMEM] + [VMEM] * (len(operands) - 1),
            out_specs=[VMEM] * len(shapes),
            compiler_params=PARAMS,
            cost_estimate=cost(64 * q_rows * rows * width, *operands),
            name=name,
        )(*operands)

    own, known = None, {}
    for step in range(1, n // 2):
        own, *known[step] = absorb(
            queries_in,
            [2 * step, 2 * step + 1],
            own,
            jnp.float32,
            f"own_far{step}",
            raw=True,
            save=True,
        )
    rest_own, other_queries, own = lax.optimization_barrier((rest_own, other_queries, own))
    rests.append(send(rest_own, 0, 1))
    theirs, other_states = absorb(
        other_queries, [2, 3], None, jnp.float32, "theirs_far1", raw=True, keep=True, given=known[1]
    )
    for step in range(2, n // 2):
        (theirs,) = absorb(
            other_states,
            [2 * step, 2 * step + 1],
            theirs,
            jnp.float32,
            f"theirs_far{step}",
            given=known[step],
        )
    (theirs,) = absorb(other_states, [0], theirs, jnp.float32, "theirs_near0")
    (theirs,) = absorb(other_states, [1], theirs, jnp.bfloat16, "theirs_near1")
    theirs_sent, own, rests[1] = lax.optimization_barrier((theirs, own, rests[1]))
    theirs = lax.ppermute(theirs_sent, "narrow", swap)
    (own,) = absorb(queries_in, [0, 1], own, jnp.float32, "own_near", raw=True)
    result = pl.pallas_call(
        finish,
        out_shape=jax.ShapeDtypeStruct((q_rows, width), jnp.bfloat16),
        in_specs=[VMEM] * 6,
        out_specs=VMEM,
        compiler_params=PARAMS,
        cost_estimate=cost(2 * q_rows * width * width, own, w_out),
        name="finish",
    )(own, theirs, gates, out_gain[None], w_out, queries_in)
    return result[None]


def solution(mesh):
    in_specs = (
        P(("parts", "wide"), "narrow", None),
        P(("parts", "wide"), "narrow", None),
        P(("parts", "wide")),
        P(("parts", "wide"), "narrow"),
        P(),
        P(),
        P(),
        P(),
        P(),
    )
    out_specs = P(("parts", "wide"), "narrow", None)
    return jax.shard_map(
        functools.partial(on_device, n=mesh.shape["narrow"], wide=mesh.shape["wide"]),
        mesh=mesh,
        in_specs=in_specs,
        out_specs=out_specs,
        check_vma=False,
    )
```

```python
import functools
import math

import jax
import jax.numpy as jnp
from jax import lax
from jax.experimental import pallas as pl
from jax.experimental.pallas import tpu as pltpu
from jax.sharding import PartitionSpec as P

SPAN = 256


def silu(x):
    half = 0.5 * x
    return half + half * jnp.tanh(half)


def pick(index, table):
    value = jnp.int32(table[0])
    for i, entry in enumerate(table[1:], 1):
        value = jnp.where(index == i, jnp.int32(entry), value)
    return value


def dot(a, b, dims=((1,), (0,))):
    return lax.dot_general(a, b, (dims, ((), ())), preferred_element_type=jnp.float32)


def project_gates(events_ref, w_ref, w_key_ref, gates_ref):
    del w_key_ref
    width = events_ref.shape[1]
    gates_ref[...] = silu(dot(events_ref[...], w_ref[:, width:]))


def pack(history_ref, labels_ref, head_ref, rest_ref, sems):
    half, width = rest_ref.shape
    copies = [
        pltpu.make_async_copy(history_ref.at[:half], head_ref.at[:half], sems.at[0]),
        pltpu.make_async_copy(history_ref.at[half:], rest_ref, sems.at[1]),
    ]
    for copy in copies:
        copy.start()
    labels = labels_ref[...].astype(jnp.float32)
    for i, at in enumerate(range(0, labels.shape[1], width)):
        part = labels[:, at : at + width]
        row = half + 16 * i
        head_ref[row : row + 16, : part.shape[1]] = jnp.broadcast_to(
            part, (16, part.shape[1])
        ).astype(jnp.bfloat16)
    for copy in copies:
        copy.wait()


def attend(length_ref, *refs, heads, parts, owners, chosen, shard_rows, first, raw, keep, save, given, scale):
    refs = list(refs)
    saved = [refs.pop() for _ in range(3)] if save else None
    kept_ref = refs.pop() if keep else None
    out_ref = refs.pop()
    total_ref = None if first else refs.pop()
    w_query_ref = refs.pop() if raw else None
    states = refs.pop()[...]
    if not given:
        table_ref, w_ref = refs.pop(), refs.pop()
    if raw:
        states = silu(dot(states, w_query_ref[:, : states.shape[1]])).astype(jnp.bfloat16)
        states = (states * scale).astype(jnp.bfloat16)
    if keep:
        kept_ref[...] = states
    place = lax.axis_index("narrow")
    owner = pick(place, owners)
    total = total_ref
    for at, rows in parts:
        if given:
            keys_ref, values_ref, bias_ref = refs
            keys, values = keys_ref[at : at + rows], values_ref[at : at + rows]
            bias = bias_ref[:, at : at + rows]
            width = keys.shape[1]
        elif chosen is None:
            hist_ref, labels_ref = refs
            hist, labels = hist_ref[at : at + rows], labels_ref[:, at : at + rows]
            width = hist.shape[1]
        else:
            take_own = pick(place, chosen) == 1
            hist = refs.pop(0)[:rows]
            even = lax.axis_index("wide") % 2 == 0
            hist = jnp.where(even, hist, refs.pop(0)[:rows])
            hist = jnp.where(take_own, refs.pop(0)[:rows], hist)
            width = hist.shape[1]
            even_labels_ref, odd_labels_ref, own_labels_ref = [refs.pop(0) for _ in range(3)]
            where = (
                slice(shard_rows // 2 + 16 * (at // width), shard_rows // 2 + 16 * (at // width) + 16),
                slice(at % width, at % width + rows),
            )
            labels = jnp.where(even, even_labels_ref[where], odd_labels_ref[where])
            labels = jnp.where(take_own, own_labels_ref[where], labels)
            labels = labels.astype(jnp.float32)[:1].astype(jnp.int32)
        head_size = width // heads
        per_span = SPAN // head_size
        q_rows = states.shape[0]
        if not given:
            start = owner * shard_rows + at
            row = start + lax.broadcasted_iota(jnp.int32, (rows, 1), 0)
            live = (row < length_ref[0]).astype(jnp.float32)
            key_value = dot(hist, w_ref[...])
            keys = silu(key_value[:, :width]).astype(jnp.bfloat16)
            values = (key_value[:, width:] * live).astype(jnp.bfloat16)
            hot = lax.broadcasted_iota(jnp.int32, (table_ref.shape[1], rows), 0) == labels
            bias = dot(table_ref[...], hot.astype(jnp.bfloat16)) * 0.5
        if save:
            saved[2][at : at + rows] = keys
            saved[1][at : at + rows] = values
            saved[0][:, at : at + rows] = bias

        lane = lax.broadcasted_iota(jnp.int32, (1, SPAN), 1) // head_size
        for block in range(width // SPAN):
            cols = slice(block * SPAN, (block + 1) * SPAN)
            queries = states[:, cols]
            stack = [queries * (lane == j).astype(jnp.bfloat16) for j in range(per_span)]
            scores = dot(jnp.concatenate(stack, axis=0), keys[:, cols], ((1,), (1,)))
            weights = []
            for j in range(per_span):
                h = block * per_span + j
                s = scores[j * q_rows : (j + 1) * q_rows] + bias[h : h + 1]
                weights.append((s + s * jnp.tanh(s)).astype(jnp.bfloat16))
            mixed = dot(jnp.concatenate(weights, axis=0), values[:, cols])
            term = mixed[:q_rows]
            for j in range(1, per_span):
                term = jnp.where(lane == j, mixed[j * q_rows : (j + 1) * q_rows], term)
            if total is not None:
                term = term + total[:, cols]
            out_ref[:, cols] = term.astype(out_ref.dtype)
        total = out_ref


def finish(total_ref, other_ref, gates_ref, gain_ref, w_ref, events_ref, out_ref):
    attended = total_ref[...] + other_ref[...].astype(jnp.float32)
    center = jnp.mean(attended, axis=-1, keepdims=True)
    away = attended - center
    spread = jnp.mean(away * away, axis=-1, keepdims=True)
    normed = away * lax.rsqrt(spread + 1e-05)
    mixed = (normed * gain_ref[...] * gates_ref[...]).astype(jnp.bfloat16)
    out_ref[...] = (events_ref[...].astype(jnp.float32) + dot(mixed, w_ref[...])).astype(jnp.bfloat16)


VMEM = pl.BlockSpec(memory_space=pltpu.VMEM)
SMEM = pl.BlockSpec(memory_space=pltpu.SMEM)
PARAMS = pltpu.CompilerParams(vmem_limit_bytes=12 * 1024 * 1024)


def routes(n):
    half = n // 2
    rank = [z if z < half else n - 1 - z for z in range(n)]

    def shard(z, step):
        own_half = (z < half) == (rank[z] % 2 == 0)
        at = (rank[z] + step) % half
        return at if own_half else n - 1 - at

    sources = []
    for step in range(half):
        row = []
        for z in range(n):
            source = shard(z, step)
            row.append(source if z < half else n - 1 - shard(n - 1 - z, step))
        sources.append(row)
    return rank, sources


def cost(flops, *arrays):
    return pl.CostEstimate(
        flops=flops,
        bytes_accessed=sum(a.size * a.dtype.itemsize for a in arrays),
        transcendentals=0,
    )


def on_device(
    hist_events, query_events, hist_lengths, time_buckets, w_key, w_query, bias_table, out_gain, w_out, *, n, wide
):
    history, queries_in, buckets = hist_events[0], query_events[0], time_buckets
    shard_rows, width = history.shape
    q_rows = queries_in.shape[0]
    heads = bias_table.shape[1]
    scale = 0.5 / math.sqrt(width // heads)
    rank, sources = routes(n)
    swap = [(z, z ^ 1) for z in range(n)]

    def send(x, step, turn=None):
        pairs = [(source, z) for z, source in enumerate(sources[step]) if source != z]
        if turn is None:
            return lax.ppermute(x, "narrow", pairs)
        lines = [i * n for i in range(wide) if i % 2 == turn]
        pairs = [(line + a, line + b) for line in lines for a, b in pairs]
        return lax.ppermute(x, ("wide", "narrow"), pairs)

    half = shard_rows // 2
    pieces = [(step, at, half) for step in range(n // 2) for at in (0, half)]
    received = {step: [send(history, step)] for step in range(1, n // 2)}
    label_rows = 16 * (-(-shard_rows // width))
    head, rest = pl.pallas_call(
        pack,
        out_shape=(
            jax.ShapeDtypeStruct((half + label_rows, width), jnp.bfloat16),
            jax.ShapeDtypeStruct((half, width), jnp.bfloat16),
        ),
        in_specs=[pl.BlockSpec(memory_space=pl.ANY), VMEM],
        out_specs=[VMEM] * 2,
        scratch_shapes=[pltpu.SemaphoreType.DMA((2,))],
        compiler_params=PARAMS,
        name="pack",
    )(history, buckets)
    queries_out, labels, head_own, rest_own = lax.optimization_barrier(
        (queries_in, buckets, head, rest)
    )
    other_queries = lax.ppermute(queries_out, "narrow", swap)
    for step in range(1, n // 2):
        received[step].append(send(labels, step))
    firsts = [send(head_own, 0, 0)]

    gates = pl.pallas_call(
        project_gates,
        out_shape=jax.ShapeDtypeStruct((q_rows, width), jnp.float32),
        in_specs=[VMEM] * 3,
        out_specs=VMEM,
        compiler_params=PARAMS,
        cost_estimate=cost(2 * q_rows * width * width, queries_in, w_query),
        name="project_gates",
    )(queries_in, w_query, w_key)
    rest_own, gates = lax.optimization_barrier((rest_own, gates))
    rests = [send(rest_own, 0, 0)]
    head_own, received[1][0] = lax.optimization_barrier((head_own, received[1][0]))
    firsts.append(send(head_own, 0, 1))

    def absorb(states, indices, total, dtype, name, raw=False, keep=False, save=False, given=None):
        step = pieces[indices[0]][0]
        parts = [pieces[index][1:] for index in indices]
        operands = [hist_lengths]
        chosen = None
        for at, _ in parts:
            if step == 0:
                chosen = [int(sources[0][z] == z) for z in range(n)]
                operands += [*rests, rest_own] if at else [*firsts, head_own]
                operands += [*firsts, head_own]
        if given is not None:
            operands += given
        elif step:
            operands += received[step]
        if given is None:
            operands += [w_key, bias_table.T]
        operands.append(states)
        if raw:
            operands.append(w_query)
        if total is not None:
            operands.append(total)
        body = functools.partial(
            attend,
            heads=heads,
            parts=parts,
            owners=sources[step],
            chosen=chosen,
            shard_rows=shard_rows,
            first=total is None,
            raw=raw,
            keep=keep,
            save=save,
            given=given is not None,
            scale=scale,
        )
        rows = sum(size for _, size in parts)
        shapes = [jax.ShapeDtypeStruct((q_rows, width), dtype)]
        if keep:
            shapes.append(jax.ShapeDtypeStruct((q_rows, width), jnp.bfloat16))
        if save:
            shapes += [jax.ShapeDtypeStruct((rows, width), jnp.bfloat16)] * 2
            shapes.append(jax.ShapeDtypeStruct((heads, rows), jnp.float32))
        return pl.pallas_call(
            body,
            out_shape=shapes,
            in_specs=[SMEM] + [VMEM] * (len(operands) - 1),
            out_specs=[VMEM] * len(shapes),
            compiler_params=PARAMS,
            cost_estimate=cost((12 if name.startswith('theirs') else 64) * q_rows * rows * width, *operands),
            name=name,
        )(*operands)

    own, known = None, {}
    for step in range(1, n // 2):
        own, *known[step] = absorb(
            queries_in,
            [2 * step, 2 * step + 1],
            own,
            jnp.float32,
            f"own_far{step}",
            raw=True,
            save=True,
        )
    rest_own, own = lax.optimization_barrier((rest_own, own))
    rests.append(send(rest_own, 0, 1))
    other_queries, own = lax.optimization_barrier((other_queries, own))
    theirs, other_states = absorb(
        other_queries, [2, 3], None, jnp.float32, "theirs_far1", raw=True, keep=True, given=known[1]
    )
    for step in range(2, n // 2):
        (theirs,) = absorb(
            other_states,
            [2 * step, 2 * step + 1],
            theirs,
            jnp.float32,
            f"theirs_far{step}",
            given=known[step],
        )
    (theirs,) = absorb(other_states, [0], theirs, jnp.float32, "theirs_near0")
    (theirs,) = absorb(other_states, [1], theirs, jnp.bfloat16, "theirs_near1")
    theirs_sent, own, rests[1] = lax.optimization_barrier((theirs, own, rests[1]))
    theirs = lax.ppermute(theirs_sent, "narrow", swap)
    (own,) = absorb(queries_in, [0, 1], own, jnp.float32, "own_near", raw=True)
    result = pl.pallas_call(
        finish,
        out_shape=jax.ShapeDtypeStruct((q_rows, width), jnp.bfloat16),
        in_specs=[VMEM] * 6,
        out_specs=VMEM,
        compiler_params=PARAMS,
        cost_estimate=cost(2 * q_rows * width * width, own, w_out),
        name="finish",
    )(own, theirs, gates, out_gain[None], w_out, queries_in)
    return result[None]


def solution(mesh):
    in_specs = (
        P(("parts", "wide"), "narrow", None),
        P(("parts", "wide"), "narrow", None),
        P(("parts", "wide")),
        P(("parts", "wide"), "narrow"),
        P(),
        P(),
        P(),
        P(),
        P(),
    )
    out_specs = P(("parts", "wide"), "narrow", None)
    return jax.shard_map(
        functools.partial(on_device, n=mesh.shape["narrow"], wide=mesh.shape["wide"]),
        mesh=mesh,
        in_specs=in_specs,
        out_specs=out_specs,
        check_vma=False,
    )
```

```python
import functools
import math

import jax
import jax.numpy as jnp
from jax import lax
from jax.experimental import pallas as pl
from jax.experimental.pallas import tpu as pltpu
from jax.sharding import PartitionSpec as P

SPAN = 256


def silu(x):
    half = 0.5 * x
    return half + half * jnp.tanh(half)


def pick(index, table):
    value = jnp.int32(table[0])
    for i, entry in enumerate(table[1:], 1):
        value = jnp.where(index == i, jnp.int32(entry), value)
    return value


def dot(a, b, dims=((1,), (0,))):
    return lax.dot_general(a, b, (dims, ((), ())), preferred_element_type=jnp.float32)


def project_gates(events_ref, w_ref, w_key_ref, gates_ref):
    del w_key_ref
    width = events_ref.shape[1]
    gates_ref[...] = silu(dot(events_ref[...], w_ref[:, width:]))


def pack(history_ref, labels_ref, head_ref, rest_ref, sems):
    half, width = rest_ref.shape
    copies = [
        pltpu.make_async_copy(history_ref.at[:half], head_ref.at[:half], sems.at[0]),
        pltpu.make_async_copy(history_ref.at[half:], rest_ref, sems.at[1]),
    ]
    for copy in copies:
        copy.start()
    labels = labels_ref[...].astype(jnp.float32)
    for i, at in enumerate(range(0, labels.shape[1], width)):
        part = labels[:, at : at + width]
        row = half + 16 * i
        head_ref[row : row + 16, : part.shape[1]] = jnp.broadcast_to(
            part, (16, part.shape[1])
        ).astype(jnp.bfloat16)
    for copy in copies:
        copy.wait()


def attend(length_ref, *refs, heads, parts, owners, chosen, shard_rows, first, raw, keep, save, given, scale):
    refs = list(refs)
    saved = [refs.pop() for _ in range(3)] if save else None
    kept_ref = refs.pop() if keep else None
    out_ref = refs.pop()
    total_ref = None if first else refs.pop()
    w_query_ref = refs.pop() if raw else None
    states = refs.pop()[...]
    if not given:
        table_ref, w_ref = refs.pop(), refs.pop()
    if raw:
        states = silu(dot(states, w_query_ref[:, : states.shape[1]])).astype(jnp.bfloat16)
        states = (states * scale).astype(jnp.bfloat16)
    if keep:
        kept_ref[...] = states
    place = lax.axis_index("narrow")
    owner = pick(place, owners)
    total = total_ref
    for at, rows in parts:
        if given:
            keys_ref, values_ref, bias_ref = refs
            keys, values = keys_ref[at : at + rows], values_ref[at : at + rows]
            bias = bias_ref[:, at : at + rows]
            width = keys.shape[1]
        elif chosen is None:
            hist_ref, labels_ref = refs
            hist, labels = hist_ref[at : at + rows], labels_ref[:, at : at + rows]
            width = hist.shape[1]
        else:
            take_own = pick(place, chosen) == 1
            hist = refs.pop(0)[:rows]
            even = lax.axis_index("wide") % 2 == 0
            hist = jnp.where(even, hist, refs.pop(0)[:rows])
            hist = jnp.where(take_own, refs.pop(0)[:rows], hist)
            width = hist.shape[1]
            even_labels_ref, odd_labels_ref, own_labels_ref = [refs.pop(0) for _ in range(3)]
            where = (
                slice(shard_rows // 2 + 16 * (at // width), shard_rows // 2 + 16 * (at // width) + 16),
                slice(at % width, at % width + rows),
            )
            labels = jnp.where(even, even_labels_ref[where], odd_labels_ref[where])
            labels = jnp.where(take_own, own_labels_ref[where], labels)
            labels = labels.astype(jnp.float32)[:1].astype(jnp.int32)
        head_size = width // heads
        per_span = SPAN // head_size
        q_rows = states.shape[0]
        if not given:
            start = owner * shard_rows + at
            row = start + lax.broadcasted_iota(jnp.int32, (rows, 1), 0)
            live = (row < length_ref[0]).astype(jnp.float32)
            key_value = dot(hist, w_ref[...])
            keys = silu(key_value[:, :width]).astype(jnp.bfloat16)
            values = (key_value[:, width:] * live).astype(jnp.bfloat16)
            hot = lax.broadcasted_iota(jnp.int32, (table_ref.shape[1], rows), 0) == labels
            bias = dot(table_ref[...], hot.astype(jnp.bfloat16)) * 0.5
        if save:
            saved[2][at : at + rows] = keys
            saved[1][at : at + rows] = values
            saved[0][:, at : at + rows] = bias

        lane = lax.broadcasted_iota(jnp.int32, (1, SPAN), 1) // head_size
        for block in range(width // SPAN):
            cols = slice(block * SPAN, (block + 1) * SPAN)
            queries = states[:, cols]
            stack = [queries * (lane == j).astype(jnp.bfloat16) for j in range(per_span)]
            scores = dot(jnp.concatenate(stack, axis=0), keys[:, cols], ((1,), (1,)))
            weights = []
            for j in range(per_span):
                h = block * per_span + j
                s = scores[j * q_rows : (j + 1) * q_rows] + bias[h : h + 1]
                weights.append((s + s * jnp.tanh(s)).astype(jnp.bfloat16))
            mixed = dot(jnp.concatenate(weights, axis=0), values[:, cols])
            term = mixed[:q_rows]
            for j in range(1, per_span):
                term = jnp.where(lane == j, mixed[j * q_rows : (j + 1) * q_rows], term)
            if total is not None:
                term = term + total[:, cols]
            out_ref[:, cols] = term.astype(out_ref.dtype)
        total = out_ref


def finish(total_ref, other_ref, gates_ref, gain_ref, w_ref, events_ref, out_ref):
    attended = total_ref[...] + other_ref[...].astype(jnp.float32)
    center = jnp.mean(attended, axis=-1, keepdims=True)
    away = attended - center
    spread = jnp.mean(away * away, axis=-1, keepdims=True)
    normed = away * lax.rsqrt(spread + 1e-05)
    mixed = (normed * gain_ref[...] * gates_ref[...]).astype(jnp.bfloat16)
    out_ref[...] = (events_ref[...].astype(jnp.float32) + dot(mixed, w_ref[...])).astype(jnp.bfloat16)


VMEM = pl.BlockSpec(memory_space=pltpu.VMEM)
SMEM = pl.BlockSpec(memory_space=pltpu.SMEM)
PARAMS = pltpu.CompilerParams(vmem_limit_bytes=12 * 1024 * 1024)


def routes(n):
    half = n // 2
    rank = [z if z < half else n - 1 - z for z in range(n)]

    def shard(z, step):
        own_half = (z < half) == (rank[z] % 2 == 0)
        at = (rank[z] + step) % half
        return at if own_half else n - 1 - at

    sources = []
    for step in range(half):
        row = []
        for z in range(n):
            source = shard(z, step)
            row.append(source if z < half else n - 1 - shard(n - 1 - z, step))
        sources.append(row)
    return rank, sources


def cost(flops, *arrays):
    return pl.CostEstimate(
        flops=flops,
        bytes_accessed=sum(a.size * a.dtype.itemsize for a in arrays),
        transcendentals=0,
    )


def on_device(
    hist_events, query_events, hist_lengths, time_buckets, w_key, w_query, bias_table, out_gain, w_out, *, n, wide
):
    history, queries_in, buckets = hist_events[0], query_events[0], time_buckets
    shard_rows, width = history.shape
    q_rows = queries_in.shape[0]
    heads = bias_table.shape[1]
    scale = 0.5 / math.sqrt(width // heads)
    rank, sources = routes(n)
    swap = [(z, z ^ 1) for z in range(n)]

    def send(x, step, turn=None):
        pairs = [(source, z) for z, source in enumerate(sources[step]) if source != z]
        if turn is None:
            return lax.ppermute(x, "narrow", pairs)
        lines = [i * n for i in range(wide) if i % 2 == turn]
        pairs = [(line + a, line + b) for line in lines for a, b in pairs]
        return lax.ppermute(x, ("wide", "narrow"), pairs)

    half = shard_rows // 2
    pieces = [(step, at, half) for step in range(n // 2) for at in (0, half)]
    received = {step: [send(history, step)] for step in range(1, n // 2)}
    label_rows = 16 * (-(-shard_rows // width))
    head, rest = pl.pallas_call(
        pack,
        out_shape=(
            jax.ShapeDtypeStruct((half + label_rows, width), jnp.bfloat16),
            jax.ShapeDtypeStruct((half, width), jnp.bfloat16),
        ),
        in_specs=[pl.BlockSpec(memory_space=pl.ANY), VMEM],
        out_specs=[VMEM] * 2,
        scratch_shapes=[pltpu.SemaphoreType.DMA((2,))],
        compiler_params=PARAMS,
        name="pack",
    )(history, buckets)
    queries_out, labels, head_own, rest_own = lax.optimization_barrier(
        (queries_in, buckets, head, rest)
    )
    other_queries = lax.ppermute(queries_out, "narrow", swap)
    for step in range(1, n // 2):
        received[step].append(send(labels, step))
    firsts = [send(head_own, 0, 0)]

    gates = pl.pallas_call(
        project_gates,
        out_shape=jax.ShapeDtypeStruct((q_rows, width), jnp.float32),
        in_specs=[VMEM] * 3,
        out_specs=VMEM,
        compiler_params=PARAMS,
        cost_estimate=cost(2 * q_rows * width * width, queries_in, w_query),
        name="project_gates",
    )(queries_in, w_query, w_key)
    rest_own, gates = lax.optimization_barrier((rest_own, gates))
    rests = [send(rest_own, 0, 0)]
    head_own, rest_own, received[1][0] = lax.optimization_barrier(
        (head_own, rest_own, received[1][0])
    )
    firsts.append(send(head_own, 0, 1))
    rests.append(send(rest_own, 0, 1))

    def absorb(states, indices, total, dtype, name, raw=False, keep=False, save=False, given=None):
        step = pieces[indices[0]][0]
        parts = [pieces[index][1:] for index in indices]
        operands = [hist_lengths]
        chosen = None
        for at, _ in parts:
            if step == 0:
                chosen = [int(sources[0][z] == z) for z in range(n)]
                operands += [*rests, rest_own] if at else [*firsts, head_own]
                operands += [*firsts, head_own]
        if given is not None:
            operands += given
        elif step:
            operands += received[step]
        if given is None:
            operands += [w_key, bias_table.T]
        operands.append(states)
        if raw:
            operands.append(w_query)
        if total is not None:
            operands.append(total)
        body = functools.partial(
            attend,
            heads=heads,
            parts=parts,
            owners=sources[step],
            chosen=chosen,
            shard_rows=shard_rows,
            first=total is None,
            raw=raw,
            keep=keep,
            save=save,
            given=given is not None,
            scale=scale,
        )
        rows = sum(size for _, size in parts)
        shapes = [jax.ShapeDtypeStruct((q_rows, width), dtype)]
        if keep:
            shapes.append(jax.ShapeDtypeStruct((q_rows, width), jnp.bfloat16))
        if save:
            shapes += [jax.ShapeDtypeStruct((rows, width), jnp.bfloat16)] * 2
            shapes.append(jax.ShapeDtypeStruct((heads, rows), jnp.float32))
        return pl.pallas_call(
            body,
            out_shape=shapes,
            in_specs=[SMEM] + [VMEM] * (len(operands) - 1),
            out_specs=[VMEM] * len(shapes),
            compiler_params=PARAMS,
            cost_estimate=cost((12 if name.startswith('theirs') else 64) * q_rows * rows * width, *operands),
            name=name,
        )(*operands)

    own, known = None, {}
    for step in range(1, n // 2):
        own, *known[step] = absorb(
            queries_in,
            [2 * step, 2 * step + 1],
            own,
            jnp.float32,
            f"own_far{step}",
            raw=True,
            save=True,
        )
    other_queries, own = lax.optimization_barrier((other_queries, own))
    theirs, other_states = absorb(
        other_queries, [2, 3], None, jnp.float32, "theirs_far1", raw=True, keep=True, given=known[1]
    )
    for step in range(2, n // 2):
        (theirs,) = absorb(
            other_states,
            [2 * step, 2 * step + 1],
            theirs,
            jnp.float32,
            f"theirs_far{step}",
            given=known[step],
        )
    (theirs,) = absorb(other_states, [0], theirs, jnp.float32, "theirs_near0")
    (theirs,) = absorb(other_states, [1], theirs, jnp.bfloat16, "theirs_near1")
    theirs_sent, own, rests[1] = lax.optimization_barrier((theirs, own, rests[1]))
    theirs = lax.ppermute(theirs_sent, "narrow", swap)
    (own,) = absorb(queries_in, [0, 1], own, jnp.float32, "own_near", raw=True)
    result = pl.pallas_call(
        finish,
        out_shape=jax.ShapeDtypeStruct((q_rows, width), jnp.bfloat16),
        in_specs=[VMEM] * 6,
        out_specs=VMEM,
        compiler_params=PARAMS,
        cost_estimate=cost(2 * q_rows * width * width, own, w_out),
        name="finish",
    )(own, theirs, gates, out_gain[None], w_out, queries_in)
    return result[None]


def solution(mesh):
    in_specs = (
        P(("parts", "wide"), "narrow", None),
        P(("parts", "wide"), "narrow", None),
        P(("parts", "wide")),
        P(("parts", "wide"), "narrow"),
        P(),
        P(),
        P(),
        P(),
        P(),
    )
    out_specs = P(("parts", "wide"), "narrow", None)
    return jax.shard_map(
        functools.partial(on_device, n=mesh.shape["narrow"], wide=mesh.shape["wide"]),
        mesh=mesh,
        in_specs=in_specs,
        out_specs=out_specs,
        check_vma=False,
    )
```

```python
import functools
import math

import jax
import jax.numpy as jnp
from jax import lax
from jax.experimental import pallas as pl
from jax.experimental.pallas import tpu as pltpu
from jax.sharding import PartitionSpec as P

SPAN = 256


def silu(x):
    half = 0.5 * x
    return half + half * jnp.tanh(half)


def pick(index, table):
    value = jnp.int32(table[0])
    for i, entry in enumerate(table[1:], 1):
        value = jnp.where(index == i, jnp.int32(entry), value)
    return value


def dot(a, b, dims=((1,), (0,))):
    return lax.dot_general(a, b, (dims, ((), ())), preferred_element_type=jnp.float32)


def project_gates(events_ref, w_ref, w_key_ref, gain_ref, gates_ref):
    del w_key_ref
    width = events_ref.shape[1]
    gates_ref[...] = silu(dot(events_ref[...], w_ref[:, width:])) * gain_ref[...]


def pack(history_ref, labels_ref, head_ref, rest_ref, sems):
    half, width = rest_ref.shape
    copies = [
        pltpu.make_async_copy(history_ref.at[:half], head_ref.at[:half], sems.at[0]),
        pltpu.make_async_copy(history_ref.at[half:], rest_ref, sems.at[1]),
    ]
    for copy in copies:
        copy.start()
    labels = labels_ref[...].astype(jnp.float32)
    for i, at in enumerate(range(0, labels.shape[1], width)):
        part = labels[:, at : at + width]
        row = half + 16 * i
        head_ref[row : row + 16, : part.shape[1]] = jnp.broadcast_to(
            part, (16, part.shape[1])
        ).astype(jnp.bfloat16)
    for copy in copies:
        copy.wait()


def attend(length_ref, *refs, heads, parts, owners, chosen, shard_rows, first, raw, keep, save, given, scale):
    refs = list(refs)
    saved = [refs.pop() for _ in range(3)] if save else None
    kept_ref = refs.pop() if keep else None
    out_ref = refs.pop()
    total_ref = None if first else refs.pop()
    w_query_ref = refs.pop() if raw else None
    states = refs.pop()[...]
    if not given:
        table_ref, w_ref = refs.pop(), refs.pop()
    if raw:
        states = silu(dot(states, w_query_ref[:, : states.shape[1]])).astype(jnp.bfloat16)
        states = (states * scale).astype(jnp.bfloat16)
    if keep:
        kept_ref[...] = states
    place = lax.axis_index("narrow")
    owner = pick(place, owners)
    total = total_ref
    for at, rows in parts:
        if given:
            keys_ref, values_ref, bias_ref = refs
            keys, values = keys_ref[at : at + rows], values_ref[at : at + rows]
            bias = bias_ref[:, at : at + rows]
            width = keys.shape[1]
        elif chosen is None:
            hist_ref, labels_ref = refs
            hist, labels = hist_ref[at : at + rows], labels_ref[:, at : at + rows]
            width = hist.shape[1]
        else:
            take_own = pick(place, chosen) == 1
            hist = refs.pop(0)[:rows]
            even = lax.axis_index("wide") % 2 == 0
            hist = jnp.where(even, hist, refs.pop(0)[:rows])
            hist = jnp.where(take_own, refs.pop(0)[:rows], hist)
            width = hist.shape[1]
            even_labels_ref, odd_labels_ref, own_labels_ref = [refs.pop(0) for _ in range(3)]
            where = (
                slice(shard_rows // 2 + 16 * (at // width), shard_rows // 2 + 16 * (at // width) + 16),
                slice(at % width, at % width + rows),
            )
            labels = jnp.where(even, even_labels_ref[where], odd_labels_ref[where])
            labels = jnp.where(take_own, own_labels_ref[where], labels)
            labels = labels.astype(jnp.float32)[:1].astype(jnp.int32)
        head_size = width // heads
        per_span = SPAN // head_size
        q_rows = states.shape[0]
        if not given:
            start = owner * shard_rows + at
            row = start + lax.broadcasted_iota(jnp.int32, (rows, 1), 0)
            live = (row < length_ref[0]).astype(jnp.float32)
            key_value = dot(hist, w_ref[...])
            keys = silu(key_value[:, :width]).astype(jnp.bfloat16)
            values = (key_value[:, width:] * live).astype(jnp.bfloat16)
            hot = lax.broadcasted_iota(jnp.int32, (table_ref.shape[1], rows), 0) == labels
            bias = dot(table_ref[...], hot.astype(jnp.bfloat16)) * 0.5
        if save:
            saved[2][at : at + rows] = keys
            saved[1][at : at + rows] = values
            saved[0][:, at : at + rows] = bias

        lane = lax.broadcasted_iota(jnp.int32, (1, SPAN), 1) // head_size
        for block in range(width // SPAN):
            cols = slice(block * SPAN, (block + 1) * SPAN)
            queries = states[:, cols]
            stack = [queries * (lane == j).astype(jnp.bfloat16) for j in range(per_span)]
            scores = dot(jnp.concatenate(stack, axis=0), keys[:, cols], ((1,), (1,)))
            weights = []
            for j in range(per_span):
                h = block * per_span + j
                s = scores[j * q_rows : (j + 1) * q_rows] + bias[h : h + 1]
                weights.append((s + s * jnp.tanh(s)).astype(jnp.bfloat16))
            mixed = dot(jnp.concatenate(weights, axis=0), values[:, cols])
            term = mixed[:q_rows]
            for j in range(1, per_span):
                term = jnp.where(lane == j, mixed[j * q_rows : (j + 1) * q_rows], term)
            if total is not None:
                term = term + total[:, cols]
            out_ref[:, cols] = term.astype(out_ref.dtype)
        total = out_ref


def finish(total_ref, other_ref, gates_ref, w_ref, events_ref, out_ref):
    attended = total_ref[...] + other_ref[...].astype(jnp.float32)
    center = jnp.mean(attended, axis=-1, keepdims=True)
    away = attended - center
    spread = jnp.mean(away * away, axis=-1, keepdims=True)
    normed = away * lax.rsqrt(spread + 1e-05)
    mixed = (normed * gates_ref[...]).astype(jnp.bfloat16)
    out_ref[...] = (events_ref[...].astype(jnp.float32) + dot(mixed, w_ref[...])).astype(jnp.bfloat16)


VMEM = pl.BlockSpec(memory_space=pltpu.VMEM)
SMEM = pl.BlockSpec(memory_space=pltpu.SMEM)
PARAMS = pltpu.CompilerParams(vmem_limit_bytes=12 * 1024 * 1024)


def routes(n):
    half = n // 2
    rank = [z if z < half else n - 1 - z for z in range(n)]

    def shard(z, step):
        own_half = (z < half) == (rank[z] % 2 == 0)
        at = (rank[z] + step) % half
        return at if own_half else n - 1 - at

    sources = []
    for step in range(half):
        row = []
        for z in range(n):
            source = shard(z, step)
            row.append(source if z < half else n - 1 - shard(n - 1 - z, step))
        sources.append(row)
    return rank, sources


def cost(flops, *arrays):
    return pl.CostEstimate(
        flops=flops,
        bytes_accessed=sum(a.size * a.dtype.itemsize for a in arrays),
        transcendentals=0,
    )


def on_device(
    hist_events, query_events, hist_lengths, time_buckets, w_key, w_query, bias_table, out_gain, w_out, *, n, wide
):
    history, queries_in, buckets = hist_events[0], query_events[0], time_buckets
    shard_rows, width = history.shape
    q_rows = queries_in.shape[0]
    heads = bias_table.shape[1]
    scale = 0.5 / math.sqrt(width // heads)
    rank, sources = routes(n)
    swap = [(z, z ^ 1) for z in range(n)]

    def send(x, step, turn=None):
        pairs = [(source, z) for z, source in enumerate(sources[step]) if source != z]
        if turn is None:
            return lax.ppermute(x, "narrow", pairs)
        lines = [i * n for i in range(wide) if i % 2 == turn]
        pairs = [(line + a, line + b) for line in lines for a, b in pairs]
        return lax.ppermute(x, ("wide", "narrow"), pairs)

    half = shard_rows // 2
    pieces = [(step, at, half) for step in range(n // 2) for at in (0, half)]
    received = {step: [send(history, step)] for step in range(1, n // 2)}
    label_rows = 16 * (-(-shard_rows // width))
    head, rest = pl.pallas_call(
        pack,
        out_shape=(
            jax.ShapeDtypeStruct((half + label_rows, width), jnp.bfloat16),
            jax.ShapeDtypeStruct((half, width), jnp.bfloat16),
        ),
        in_specs=[pl.BlockSpec(memory_space=pl.ANY), VMEM],
        out_specs=[VMEM] * 2,
        scratch_shapes=[pltpu.SemaphoreType.DMA((2,))],
        compiler_params=PARAMS,
        name="pack",
    )(history, buckets)
    queries_out, labels, head_own, rest_own = lax.optimization_barrier(
        (queries_in, buckets, head, rest)
    )
    other_queries = lax.ppermute(queries_out, "narrow", swap)
    for step in range(1, n // 2):
        received[step].append(send(labels, step))
    firsts = [send(head_own, 0, 0)]

    gates = pl.pallas_call(
        project_gates,
        out_shape=jax.ShapeDtypeStruct((q_rows, width), jnp.float32),
        in_specs=[VMEM] * 4,
        out_specs=VMEM,
        compiler_params=PARAMS,
        cost_estimate=cost(2 * q_rows * width * width, queries_in, w_query),
        name="project_gates",
    )(queries_in, w_query, w_key, out_gain[None])
    rest_own, gates = lax.optimization_barrier((rest_own, gates))
    rests = [send(rest_own, 0, 0)]
    head_own, rest_own, received[1][0] = lax.optimization_barrier(
        (head_own, rest_own, received[1][0])
    )
    firsts.append(send(head_own, 0, 1))
    rests.append(send(rest_own, 0, 1))

    def absorb(states, indices, total, dtype, name, raw=False, keep=False, save=False, given=None):
        step = pieces[indices[0]][0]
        parts = [pieces[index][1:] for index in indices]
        operands = [hist_lengths]
        chosen = None
        for at, _ in parts:
            if step == 0:
                chosen = [int(sources[0][z] == z) for z in range(n)]
                operands += [*rests, rest_own] if at else [*firsts, head_own]
                operands += [*firsts, head_own]
        if given is not None:
            operands += given
        elif step:
            operands += received[step]
        if given is None:
            operands += [w_key, bias_table.T]
        operands.append(states)
        if raw:
            operands.append(w_query)
        if total is not None:
            operands.append(total)
        body = functools.partial(
            attend,
            heads=heads,
            parts=parts,
            owners=sources[step],
            chosen=chosen,
            shard_rows=shard_rows,
            first=total is None,
            raw=raw,
            keep=keep,
            save=save,
            given=given is not None,
            scale=scale,
        )
        rows = sum(size for _, size in parts)
        shapes = [jax.ShapeDtypeStruct((q_rows, width), dtype)]
        if keep:
            shapes.append(jax.ShapeDtypeStruct((q_rows, width), jnp.bfloat16))
        if save:
            shapes += [jax.ShapeDtypeStruct((rows, width), jnp.bfloat16)] * 2
            shapes.append(jax.ShapeDtypeStruct((heads, rows), jnp.float32))
        return pl.pallas_call(
            body,
            out_shape=shapes,
            in_specs=[SMEM] + [VMEM] * (len(operands) - 1),
            out_specs=[VMEM] * len(shapes),
            compiler_params=PARAMS,
            cost_estimate=cost((12 if name.startswith('theirs') else 64) * q_rows * rows * width, *operands),
            name=name,
        )(*operands)

    own, known = None, {}
    for step in range(1, n // 2):
        own, *known[step] = absorb(
            queries_in,
            [2 * step, 2 * step + 1],
            own,
            jnp.float32,
            f"own_far{step}",
            raw=True,
            save=True,
        )
    other_queries, own = lax.optimization_barrier((other_queries, own))
    theirs, other_states = absorb(
        other_queries, [2, 3], None, jnp.float32, "theirs_far1", raw=True, keep=True, given=known[1]
    )
    for step in range(2, n // 2):
        (theirs,) = absorb(
            other_states,
            [2 * step, 2 * step + 1],
            theirs,
            jnp.float32,
            f"theirs_far{step}",
            given=known[step],
        )
    (theirs,) = absorb(other_states, [0], theirs, jnp.float32, "theirs_near0")
    (theirs,) = absorb(other_states, [1], theirs, jnp.bfloat16, "theirs_near1")
    theirs_sent, own, rests[1] = lax.optimization_barrier((theirs, own, rests[1]))
    theirs = lax.ppermute(theirs_sent, "narrow", swap)
    (own,) = absorb(queries_in, [0, 1], own, jnp.float32, "own_near", raw=True)
    result = pl.pallas_call(
        finish,
        out_shape=jax.ShapeDtypeStruct((q_rows, width), jnp.bfloat16),
        in_specs=[VMEM] * 5,
        out_specs=VMEM,
        compiler_params=PARAMS,
        cost_estimate=cost(2 * q_rows * width * width, own, w_out),
        name="finish",
    )(own, theirs, gates, w_out, queries_in)
    return result[None]


def solution(mesh):
    in_specs = (
        P(("parts", "wide"), "narrow", None),
        P(("parts", "wide"), "narrow", None),
        P(("parts", "wide")),
        P(("parts", "wide"), "narrow"),
        P(),
        P(),
        P(),
        P(),
        P(),
    )
    out_specs = P(("parts", "wide"), "narrow", None)
    return jax.shard_map(
        functools.partial(on_device, n=mesh.shape["narrow"], wide=mesh.shape["wide"]),
        mesh=mesh,
        in_specs=in_specs,
        out_specs=out_specs,
        check_vma=False,
    )
```
